32 devices in a mesh: lon: 8 (over y, x, core), lat: 4 (over z).
Axes of the slice: x: 2, y: 2, z: 4, core: 2. Of those that a mesh axis runs over, the one named last changes fastest.
Arguments:
- queries: bfloat16 [32, 128, 1536], P('lat', 'lon'), may hold values from -24 to 24
- keys: bfloat16 [32, 128, 1536], P('lat', 'lon'), may hold values from -24 to 24
- values: bfloat16 [32, 128, 1536], P('lat', 'lon'), may hold values from -6 to 6
- out_grad: bfloat16 [32, 128, 1536], P('lat', 'lon'), may hold values from -6 to 6
- neighbours: int32 [32, 5], replicated, may hold values from -1 to 31, as said below
- partner: int32 [2, 8], replicated, may hold values from 0 to 7, as said below
Outputs:
- attended: bfloat16 [32, 128, 1536], P('lat', 'lon')
- grad_queries: bfloat16 [32, 128, 1536], P('lat', 'lon')
- grad_keys: bfloat16 [32, 128, 1536], P('lat', 'lon')
- grad_values: bfloat16 [32, 128, 1536], P('lat', 'lon')
The draws below stay inside these ranges and needn't reach their ends.
Inputs may be any that keep to these rules, and one draw needn't show every extreme that they name: `neighbours`: row t = b * 8 + s lists, in some order and padded with -1, distinct tiles: t itself always, and any of b * 8 + (s - 1) mod 8, b * 8 + (s + 1) mod 8, t - 8 where b > 0 and t + 8 where b < 3. Rows of the first and the last band list all of those that exist. Each row is a permutation of the strips, and partner[j, s] - s - 4 is -1, 0 or 1 modulo 8.
All inputs are finite; a program needn't handle non-finite values.
Results may differ from the reference program's by a relative error of at most 0.022.
Values may be sent and summed in bfloat16 or wider, within the bound.
No kernel may reach another device: no remote copies, remote signals or barrier semaphores. Data moves between devices by JAX's collectives and lax.ppermute only.
A program may use at most 64 MiB of HBM per device.

```python
import jax
import jax.numpy as jnp
from jax import lax

H = 12
DH = 128
TR = 8
TC = 16
HD = 1536
STRIPS = 8
BANDS = 4
TILES = 32
ROWS = 32
COLS = 128


def query_key_pair(key):
    base = jax.random.fold_in(key, 31)
    first, second = jax.random.split(base, 2)
    shape = (ROWS, COLS, H, DH)
    query_vals = jnp.clip(jax.random.normal(first, shape, jnp.float32), -4.0, 4.0)
    key_vals = jnp.clip(jax.random.normal(second, shape, jnp.float32), -4.0, 4.0)
    query_vals = query_vals.reshape(ROWS, COLS, H * DH).astype(jnp.bfloat16)
    key_vals = key_vals.reshape(ROWS, COLS, H * DH).astype(jnp.bfloat16)
    return (query_vals, key_vals)


def draw_queries(key, part):
    return query_key_pair(key)[0]


def draw_keys(key, part):
    return query_key_pair(key)[1]


def draw_neighbours(key, part):
    base = jax.random.fold_in(key, 47)
    keep_key, order_key = jax.random.split(base, 2)
    band_ids = jnp.arange(BANDS)[:, None]
    strip_ids = jnp.arange(STRIPS)[None, :]
    own_ids = band_ids * STRIPS + strip_ids
    west_ids = band_ids * STRIPS + (strip_ids - 1) % STRIPS
    east_ids = band_ids * STRIPS + (strip_ids + 1) % STRIPS
    north_ids = jnp.where(band_ids > 0, own_ids - STRIPS, -1)
    south_ids = jnp.where(band_ids < BANDS - 1, own_ids + STRIPS, -1)
    polar_band = (band_ids == 0) | (band_ids == BANDS - 1)
    keeping = jax.random.randint(keep_key, (BANDS, STRIPS, 4), 0, 2)
    keeping = jnp.where(polar_band[:, :, None], 1, keeping)
    others = jnp.stack([west_ids, east_ids, north_ids, south_ids], axis=-1)
    others = jnp.where(keeping == 1, others, -1)
    table = jnp.concatenate([own_ids[:, :, None], others], axis=-1).reshape(TILES, 5)
    ranking = jax.random.randint(order_key, (TILES, 5), 0, 1 << 20) * 8 + jnp.arange(5)[None, :]
    ordering = jnp.argsort(ranking, axis=1)
    return jnp.take_along_axis(table, ordering, axis=1).astype(jnp.int32)


def draw_partner(key, part):
    base = jax.random.fold_in(key, 59)
    phase_key, flip_key = jax.random.split(base, 2)
    phase = jax.random.randint(phase_key, (), 0, 2)
    flipping = jax.random.randint(flip_key, (2, STRIPS // 2), 0, 2)
    strip_ids = jnp.arange(STRIPS)
    shifted = (strip_ids - phase) % STRIPS
    pair_ids = shifted // 2
    leading = shifted % 2 == 0
    flip_on = flipping[:, pair_ids]
    offsets = jnp.where(flip_on == 1, jnp.where(leading, 1, -1), 0)
    return ((strip_ids[None, :] + offsets + STRIPS // 2) % STRIPS).astype(jnp.int32)


def level_of(stream_key, extent, cuts, smallest, largest):
    factor_of = 1.0
    for dim, parts in cuts:
        draws = jax.random.uniform(jax.random.fold_in(jax.random.fold_in(stream_key, 6), dim), (parts,), jnp.float32, smallest / len(cuts), largest / len(cuts))
        factor_of = factor_of * jnp.repeat(jnp.exp(draws), extent[dim] // parts).reshape((-1,) + (1,) * (len(extent) - 1 - dim))
    return factor_of


def scatter_about(rng, shape, spread, limit, pieces=(), kind=jnp.bfloat16):
    level = level_of(rng, shape, pieces, -0.22, 0.18) if pieces else 1.0
    result = jax.random.normal(rng, shape, jnp.float32) * spread * level
    return jnp.minimum(jnp.maximum(result, -limit), limit).astype(kind)


def setup_inputs(seed: int = 0) -> dict:
    splits = jax.random.split(jax.random.key(seed), 7)
    queries = draw_queries(jax.random.fold_in(splits[6], 71), 0)
    keys = draw_keys(jax.random.fold_in(splits[6], 71), 0)
    values = scatter_about(splits[2], (ROWS, COLS, HD), 1.0, 6.0, ((0, 4), (1, 8)))
    out_grad = scatter_about(splits[3], (ROWS, COLS, HD), 1.0, 6.0, ((0, 4), (1, 8)))
    neighbours = draw_neighbours(jax.random.fold_in(splits[6], 71), 0)
    partner = draw_partner(jax.random.fold_in(splits[6], 71), 0)
    return {"queries": queries, "keys": keys, "values": values, "out_grad": out_grad, "neighbours": neighbours, "partner": partner}


def to_tiles(array):
    shaped = array.reshape(BANDS, TR, STRIPS, TC, H, DH).transpose(0, 2, 1, 3, 4, 5)
    return shaped.reshape(BANDS * STRIPS, TR * TC, H, DH)


def from_tiles(array):
    shaped = array.reshape(BANDS, STRIPS, TR, TC, H * DH).transpose(0, 2, 1, 3, 4)
    return shaped.reshape(TR * BANDS, TC * STRIPS, H * DH)


def reference(queries, keys, values, out_grad, neighbours, partner):
    scale = DH ** -0.5
    tile_query = to_tiles(queries)
    tile_key = to_tiles(keys)
    tile_value = to_tiles(values)
    tile_grad = to_tiles(out_grad)

    def per_tile(carry, index):
        key_total, value_total = carry
        band_id = index // STRIPS
        strip_id = index % STRIPS
        partner_row = jnp.where(band_id == 0, partner[0], partner[1])
        polar_band = (band_id == 0) | (band_id == BANDS - 1)
        extra = jnp.where(polar_band, band_id * STRIPS + partner_row[strip_id], -1).astype(jnp.int32)
        links = jnp.concatenate([neighbours[index].astype(jnp.int32), extra[None]])
        valid = links >= 0
        safe = jnp.where(valid, links, 0).astype(jnp.int32)
        near_keys = tile_key[safe].astype(jnp.float32)
        near_values = tile_value[safe].astype(jnp.float32)
        query = tile_query[index].astype(jnp.float32)
        cotan = tile_grad[index].astype(jnp.float32)
        scores = jnp.einsum('qhd,jkhd->hqjk', query, near_keys) * scale
        scores = jnp.where(valid[None, None, :, None], scores, -jnp.inf)
        highest = jnp.max(scores, axis=(2, 3), keepdims=True)
        total = jnp.sum(jnp.exp(scores - highest), axis=(2, 3), keepdims=True)
        log_norm = highest + jnp.log(total)
        probability = jnp.exp(scores - log_norm)
        weights = probability.astype(jnp.bfloat16).astype(jnp.float32)
        attended = jnp.einsum('hqjk,jkhd->qhd', weights, near_values).astype(jnp.bfloat16)
        delta = jnp.sum(cotan * attended.astype(jnp.float32), axis=-1)
        dprob = jnp.einsum('qhd,jkhd->hqjk', cotan, near_values)
        dscore = (probability * (dprob - delta.T[:, :, None, None])).astype(jnp.bfloat16).astype(jnp.float32)
        grad_query = (scale * jnp.einsum('hqjk,jkhd->qhd', dscore, near_keys)).astype(jnp.bfloat16)
        key_part = jnp.einsum('hqjk,qhd->jkhd', dscore, query)
        value_part = jnp.einsum('hqjk,qhd->jkhd', weights, cotan)
        key_total = key_total.at[safe].add(key_part)
        value_total = value_total.at[safe].add(value_part)
        return (key_total, value_total), (attended, grad_query)

    empty = jnp.zeros((BANDS * STRIPS, TR * TC, H, DH), jnp.float32)
    (key_total, value_total), (attended, grad_query) = lax.scan(
        per_tile, (empty, empty), jnp.arange(BANDS * STRIPS, dtype=jnp.int32))
    grad_keys = (scale * key_total).astype(jnp.bfloat16)
    grad_values = value_total.astype(jnp.bfloat16)
    return from_tiles(attended), from_tiles(grad_query), from_tiles(grad_keys), from_tiles(grad_values)
```

```python
import functools
import math

import jax
import jax.numpy as jnp
from jax import lax
from jax.experimental import pallas as pl
from jax.experimental.pallas import tpu as pltpu
from jax.sharding import PartitionSpec as P

DH = 128
CHUNKS = 1
STEP_HEADS = 2
LOW = -1e30
F32 = jnp.float32
BF16 = jnp.bfloat16


def dot_nt(a, b):
    return lax.dot_general(a, b, (((1,), (1,)), ((), ())), preferred_element_type=F32)


def dot_nn(a, b):
    return lax.dot_general(a, b, (((1,), (0,)), ((), ())), preferred_element_type=F32)


def dot_tn(a, b):
    return lax.dot_general(a, b, (((0,), (0,)), ((), ())), preferred_element_type=F32)


def rows(*parts):
    return jnp.concatenate(parts, axis=0)


def block_bias(flags, slot, tokens, both):
    own = jnp.where(flags[slot] > 0, 0.0, LOW).astype(F32)
    if not both:
        return jnp.full((1, tokens), own, F32)
    other = jnp.where(flags[8 + slot] > 0, 0.0, LOW).astype(F32)
    lane = lax.broadcasted_iota(jnp.int32, (1, 2 * tokens), 1)
    return jnp.where(lane < tokens, own, other)


def gathered(j, polar, q, k, v, g, near):
    cols = pl.ds(j * DH, DH)
    slots = near[:3] if polar else near
    kk = rows(k[:, cols], *[r[0, :, cols] for r in slots])
    vv = rows(v[:, cols], *[r[1, :, cols] for r in slots])
    qq, gg = q[:, cols], g[:, cols]
    if polar:
        qq = rows(qq, near[3][0, :, cols])
        gg = rows(gg, near[3][1, :, cols])
    return qq, gg, kk, vv


def stats_kernel(factor, heads, tokens, flags, q, k, v, g, n1, n2, n3, n4, out):
    near = (n1, n2, n3, n4)

    def work(polar):
        width = 2 * tokens if polar else tokens
        count = 4 if polar else 5
        bias = [block_bias(flags, b, tokens, polar) for b in range(count)]
        tops, sums, deltas = [], [], []
        for j in range(heads):
            qq, gg, kk, vv = gathered(j, polar, q, k, v, g, near)
            s = dot_nt(kk, qq)
            dp = dot_nt(vv, gg)
            parts = [s[b * tokens : (b + 1) * tokens] * factor + bias[b] for b in range(count)]
            top = functools.reduce(jnp.maximum, [jnp.max(x, axis=0, keepdims=True) for x in parts])
            total = jnp.zeros((1, width), F32)
            delta = jnp.zeros((1, width), F32)
            for b in range(count):
                e = jnp.exp2(parts[b] - top)
                total += jnp.sum(e, axis=0, keepdims=True)
                delta += jnp.sum(e * dp[b * tokens : (b + 1) * tokens], axis=0, keepdims=True)
            tops.append(top)
            sums.append(total)
            deltas.append(delta)
        stat = rows(*tops, *sums, *deltas)
        for r in range(3 * heads):
            out[0, r : r + 1, :width] = stat[r : r + 1]
        if out.shape[1] > 3 * heads:
            out[0, 3 * heads :, :] = jnp.zeros((out.shape[1] - 3 * heads, 2 * tokens), F32)
        if not polar:
            out[0, : 3 * heads, tokens:] = jnp.zeros((3 * heads, tokens), F32)

    pl.when(flags[7] > 0)(lambda: work(True))
    pl.when(flags[7] == 0)(lambda: work(False))


def grads_kernel(factor, heads, tokens, flags, mine, theirs, q, k, v, g, n1, n2, n3, n4, att, dq, dk, dv, r1, r2, r3, r4):
    near = (n1, n2, n3, n4)
    back = (r1, r2, r3, r4)

    def work(polar):
        width = 2 * tokens if polar else tokens
        count = 4 if polar else 5
        bias = [block_bias(flags, b, tokens, polar) for b in range(count)]
        for j in range(heads):
            cols = pl.ds(j * DH, DH)
            top, total, delta = [mine[0, r * heads + j : r * heads + j + 1, :width] for r in range(3)]
            if polar:
                top2, total2, delta2 = [
                    jnp.concatenate(
                        [
                            theirs[0, r * heads + j : r * heads + j + 1, tokens:],
                            theirs[0, r * heads + j : r * heads + j + 1, :tokens],
                        ],
                        axis=1,
                    )
                    for r in range(3)
                ]
                high = jnp.maximum(top, top2)
                a1, a2 = jnp.exp2(top - high), jnp.exp2(top2 - high)
                total = total * a1 + total2 * a2
                delta = delta * a1 + delta2 * a2
                top = high
            lse = top + jnp.log2(total)
            delta = delta / total
            qq, gg, kk, vv = gathered(j, polar, q, k, v, g, near)
            s = dot_nt(kk, qq)
            dp = dot_nt(vv, gg)
            ps = []
            for b in range(count):
                ps.append(jnp.exp2(s[b * tokens : (b + 1) * tokens] * factor + (bias[b] - lse)))
            p = rows(*ps)
            w = p.astype(BF16)
            ds = (p * (dp - delta)).astype(BF16)
            dkk = dot_nn(ds, qq)
            dvv = dot_nn(w, gg)
            o = dot_tn(vv, w).T
            dqq = dot_tn(kk, ds).T
            att[:, cols] = o[:tokens]
            dq[:, cols] = dqq[:tokens]
            dk[:, cols] = dkk[:tokens]
            dv[:, cols] = dvv[:tokens]
            for b in range(1, count):
                back[b - 1][0, :, cols] = dkk[b * tokens : (b + 1) * tokens].astype(BF16)
                back[b - 1][1, :, cols] = dvv[b * tokens : (b + 1) * tokens].astype(BF16)
            if polar:
                r4[0, :, cols] = o[tokens:].astype(BF16)
                r4[1, :, cols] = dqq[tokens:].astype(BF16)

    pl.when(flags[7] > 0)(lambda: work(True))
    pl.when(flags[7] == 0)(lambda: work(False))


def exchange_plan(lon_count, lat_count):
    half = lon_count // 2

    def polar(b):
        return b == 0 or b == lat_count - 1

    def second(b, s):
        ring, base = (half, s // half * half) if polar(b) else (lon_count, 0)
        place = s - base
        return base + (place - 1 if place % 2 == 0 else place + 1) % ring

    def fourth(b, s):
        if polar(b):
            return b, (s + half) % lon_count
        return (b - 1 if b % 2 == 0 else b + 1), s

    cells = [(b, s) for b in range(lat_count) for s in range(lon_count)]

    def pairs(move, chosen=cells):
        return [(s * lat_count + b, move(b, s)[1] * lat_count + move(b, s)[0]) for b, s in chosen]

    return (
        pairs(lambda b, s: (b, s ^ 1)),
        pairs(lambda b, s: (b, second(b, s))),
        pairs(lambda b, s: (b ^ 1, s)),
        pairs(fourth),
        pairs(fourth, [(b, s) for b, s in cells if polar(b)]),
    )


def link_flags(neighbours, partner, lon_count, lat_count):
    half = lon_count // 2
    b, s = lax.axis_index("lat"), lax.axis_index("lon")
    polar = (b == 0) | (b == lat_count - 1)
    first = s ^ 1
    ring = jnp.where(polar, half, lon_count)
    base = jnp.where(polar, s // half * half, 0)
    place = s - base
    second = base + (place + jnp.where(place % 2 == 0, ring - 1, 1)) % ring
    inner = jnp.where(b % 2 == 0, b - 1, b + 1)
    held = jnp.stack([
        b * lon_count + s,
        b * lon_count + first,
        b * lon_count + second,
        (b ^ 1) * lon_count + s,
        jnp.where(polar, -7, inner * lon_count + s),
    ])
    across = (s + half) % lon_count
    pole = jnp.where(b == 0, partner[0], partner[1])

    def links(strip):
        tile = b * lon_count + strip
        extra = jnp.where(polar, b * lon_count + pole[strip], -9)
        return jnp.concatenate([neighbours[tile], extra[None]])

    own = jnp.any(held[:, None] == links(s)[None, :], axis=1)
    other = jnp.any(held[:3, None] == links(across)[None, :], axis=1)
    parts = [own, jnp.zeros((2,), bool), polar[None], other, jnp.zeros((5,), bool)]
    return jnp.concatenate(parts).astype(jnp.int32), polar


def body(queries, keys, values, out_grad, neighbours, partner):
    lat_count, lon_count = lax.axis_size("lat"), lax.axis_size("lon")
    tile_rows, tile_cols, features = queries.shape
    tokens = tile_rows * tile_cols
    heads = features // DH
    scale = DH**-0.5
    factor = scale * math.log2(math.e)
    q, k, v, g = [x.reshape(tokens, features) for x in (queries, keys, values, out_grad)]
    p1, p2, p3, p4, swap = exchange_plan(lon_count, lat_count)
    axes = ("lon", "lat")
    flags, polar = link_flags(neighbours, partner, lon_count, lat_count)

    chunk_heads = heads // CHUNKS
    step_heads = STEP_HEADS
    steps = chunk_heads // step_heads
    wide = chunk_heads * DH
    block = step_heads * DH
    stat_rows = -(-3 * step_heads // 8) * 8
    params = pltpu.CompilerParams(vmem_limit_bytes=48 * 1024 * 1024)

    def compute(c, near):
        own = pl.BlockSpec((tokens, block), lambda i, f: (0, c * steps + i))
        pair = pl.BlockSpec((2, tokens, block), lambda i, f: (0, 0, i))
        flat = pl.BlockSpec((tokens, block), lambda i, f: (0, i))
        stat = pl.BlockSpec((1, stat_rows, 2 * tokens), lambda i, f: (i, 0, 0))
        stats = pl.pallas_call(
            functools.partial(stats_kernel, factor, step_heads, tokens),
            grid_spec=pltpu.PrefetchScalarGridSpec(
                num_scalar_prefetch=1,
                grid=(steps,),
                in_specs=[own] * 4 + [pair] * 4,
                out_specs=stat,
            ),
            out_shape=jax.ShapeDtypeStruct((steps, stat_rows, 2 * tokens), F32),
            compiler_params=params,
            name="stats",
        )(flags, q, k, v, g, *near)
        swapped = lax.ppermute(stats, axes, swap)
        whole = jax.ShapeDtypeStruct((tokens, wide), F32)
        term = jax.ShapeDtypeStruct((2, tokens, wide), BF16)
        return pl.pallas_call(
            functools.partial(grads_kernel, factor, step_heads, tokens),
            grid_spec=pltpu.PrefetchScalarGridSpec(
                num_scalar_prefetch=1,
                grid=(steps,),
                in_specs=[stat] * 2 + [own] * 4 + [pair] * 4,
                out_specs=[flat] * 4 + [pair] * 4,
            ),
            out_shape=[whole] * 4 + [term] * 4,
            compiler_params=params,
            name="grads",
        )(flags, stats, swapped, q, k, v, g, *near)

    outs = []
    for c in range(CHUNKS):
        cut = slice(c * wide, (c + 1) * wide)
        kv = jnp.stack([k[:, cut], v[:, cut]])
        qg = jnp.stack([q[:, cut], g[:, cut]])
        n1, n2, n3 = [lax.ppermute(kv, axes, p) for p in (p1, p2, p3)]
        n4 = lax.ppermute(jnp.where(polar, qg, kv), axes, p4)
        att, dq, dk, dv, t1, t2, t3, t4 = compute(c, (n1, n2, n3, n4))
        b1, b2, b3, b4 = [lax.ppermute(t, axes, p).astype(F32) for t, p in zip((t1, t2, t3, t4), (p1, p2, p3, p4))]
        fourth_q = jnp.where(polar, b4, 0.0)
        fourth_k = jnp.where(polar, 0.0, b4)
        outs.append((
            (att + fourth_q[0]).astype(BF16),
            (scale * (dq + fourth_q[1])).astype(BF16),
            (scale * (dk + b1[0] + b2[0] + b3[0] + fourth_k[0])).astype(BF16),
            (dv + b1[1] + b2[1] + b3[1] + fourth_k[1]).astype(BF16),
        ))
    shape = (tile_rows, tile_cols, features)
    return tuple(
        (parts[0] if CHUNKS == 1 else jnp.concatenate(parts, axis=1)).reshape(shape) for parts in zip(*outs)
    )


def solution(mesh):
    spec = P("lat", "lon", None)
    return jax.shard_map(
        body,
        mesh=mesh,
        in_specs=(spec,) * 4 + (P(),) * 2,
        out_specs=(spec,) * 4,
        check_vma=False,
    )
```

```python
import functools
import math

import jax
import jax.numpy as jnp
from jax import lax
from jax.experimental import pallas as pl
from jax.experimental.pallas import tpu as pltpu
from jax.sharding import PartitionSpec as P

DH = 128
SHARES = (0, 6, 12)
FINISH_WIDTH = 0
AHEAD = True
ORDER = (3, 1, 2, 0)
TIES = ((3,), (0,), (3,), (0,))
LATE = (0, 1, 2)
LAST = ((2,), (), (), ())
VMEM_BYTES = 16 * 1024 * 1024
SCALE = DH**-0.5
FACTOR = SCALE * math.log2(math.e)
LOW = -1e30
F32 = jnp.float32
BF16 = jnp.bfloat16


def dot_nt(a, b):
    return lax.dot_general(a, b, (((1,), (1,)), ((), ())), preferred_element_type=F32)


def dot_nn(a, b):
    return lax.dot_general(a, b, (((1,), (0,)), ((), ())), preferred_element_type=F32)


def dot_tn(a, b):
    return lax.dot_general(a, b, (((0,), (0,)), ((), ())), preferred_element_type=F32)


def rows(*parts):
    return jnp.concatenate(parts, axis=0)


def block_bias(flags, slot, tokens, both):
    own = jnp.where(flags[slot] > 0, 0.0, LOW).astype(F32)
    if not both:
        return jnp.full((1, tokens), own, F32)
    other = jnp.where(flags[8 + slot] > 0, 0.0, LOW).astype(F32)
    lane = lax.broadcasted_iota(jnp.int32, (1, 2 * tokens), 1)
    return jnp.where(lane < tokens, own, other)


def gathered(j, polar, qg, kv, near):
    cols = pl.ds(j * DH, DH)
    slots = (kv,) + (near[:3] if polar else near)
    kk, vv = [rows(*[r[i, :, cols] for r in slots]) for i in range(2)]
    qq, gg = [rows(qg[i, :, cols], near[3][i, :, cols]) if polar else qg[i, :, cols] for i in range(2)]
    return qq, gg, kk, vv


def stats_kernel(heads, tokens, flags, n4, n2, n3, n1, qg, kv, out):
    near = (n1, n2, n3, n4)

    def work(polar):
        width = 2 * tokens if polar else tokens
        count = 4 if polar else 5
        bias = [block_bias(flags, b, tokens, polar) for b in range(count)]
        tops, sums, deltas = [], [], []
        for j in range(heads):
            qq, gg, kk, vv = gathered(j, polar, qg, kv, near)
            s = dot_nt(kk, qq)
            dp = dot_nt(vv, gg)
            parts = [s[b * tokens : (b + 1) * tokens] * FACTOR + bias[b] for b in range(count)]
            top = functools.reduce(jnp.maximum, [jnp.max(x, axis=0, keepdims=True) for x in parts])
            total = jnp.zeros((1, width), F32)
            delta = jnp.zeros((1, width), F32)
            for b in range(count):
                e = jnp.exp2(parts[b] - top)
                total += jnp.sum(e, axis=0, keepdims=True)
                delta += jnp.sum(e * dp[b * tokens : (b + 1) * tokens], axis=0, keepdims=True)
            tops.append(top)
            sums.append(total)
            deltas.append(delta)
        stat = rows(*tops, *sums, *deltas)
        for r in range(3 * heads):
            out[r : r + 1, :width] = stat[r : r + 1]
        if out.shape[0] > 3 * heads:
            out[3 * heads :, :] = jnp.zeros((out.shape[0] - 3 * heads, 2 * tokens), F32)
        if not polar:
            out[: 3 * heads, tokens:] = jnp.zeros((3 * heads, tokens), F32)

    pl.when(flags[7] > 0)(lambda: work(True))
    pl.when(flags[7] == 0)(lambda: work(False))


def grads_kernel(heads, tokens, flags, n4, n2, n3, n1, mine, theirs, qg, kv, att, dq, dk, dv, r1, r2, r3, r4):
    near = (n1, n2, n3, n4)
    back = (r1, r2, r3, r4)

    def work(polar):
        width = 2 * tokens if polar else tokens
        count = 4 if polar else 5
        bias = [block_bias(flags, b, tokens, polar) for b in range(count)]
        for j in range(heads):
            cols = pl.ds(j * DH, DH)
            top, total, delta = [mine[r * heads + j : r * heads + j + 1, :width] for r in range(3)]
            if polar:
                top2, total2, delta2 = [
                    jnp.concatenate(
                        [
                            theirs[r * heads + j : r * heads + j + 1, tokens:],
                            theirs[r * heads + j : r * heads + j + 1, :tokens],
                        ],
                        axis=1,
                    )
                    for r in range(3)
                ]
                high = jnp.maximum(top, top2)
                a1, a2 = jnp.exp2(top - high), jnp.exp2(top2 - high)
                total = total * a1 + total2 * a2
                delta = delta * a1 + delta2 * a2
                top = high
            lse = top + jnp.log2(total)
            delta = delta / total
            qq, gg, kk, vv = gathered(j, polar, qg, kv, near)
            s = dot_nt(kk, qq)
            dp = dot_nt(vv, gg)
            ps = []
            for b in range(count):
                ps.append(jnp.exp2(s[b * tokens : (b + 1) * tokens] * FACTOR + (bias[b] - lse)))
            p = rows(*ps)
            w = p.astype(BF16)
            ds = (p * (dp - delta)).astype(BF16)
            dkk = dot_nn(ds, qq)
            dvv = dot_nn(w, gg)
            o = dot_tn(vv, w).T
            dqq = dot_tn(kk, ds).T
            att[:, cols] = o[:tokens]
            dq[:, cols] = dqq[:tokens]
            dk[:, cols] = dkk[:tokens]
            dv[:, cols] = dvv[:tokens]
            for b in range(1, count):
                back[b - 1][0, :, cols] = dkk[b * tokens : (b + 1) * tokens].astype(BF16)
                back[b - 1][1, :, cols] = dvv[b * tokens : (b + 1) * tokens].astype(BF16)
            if polar:
                r4[0, :, cols] = o[tokens:].astype(BF16)
                r4[1, :, cols] = dqq[tokens:].astype(BF16)

    pl.when(flags[7] > 0)(lambda: work(True))
    pl.when(flags[7] == 0)(lambda: work(False))


def exchange_plan(lon_count, lat_count):
    half = lon_count // 2

    def polar(b):
        return b == 0 or b == lat_count - 1

    def second(b, s):
        ring, base = (half, s // half * half) if polar(b) else (lon_count, 0)
        place = s - base
        return base + (place - 1 if place % 2 == 0 else place + 1) % ring

    def fourth(b, s):
        if polar(b):
            return b, (s + half) % lon_count
        return (b - 1 if b % 2 == 0 else b + 1), s

    cells = [(b, s) for b in range(lat_count) for s in range(lon_count)]

    def pairs(move):
        return [(s * lat_count + b, move(b, s)[1] * lat_count + move(b, s)[0]) for b, s in cells]

    return (
        pairs(lambda b, s: (b, s ^ 1)),
        pairs(lambda b, s: (b, second(b, s))),
        pairs(lambda b, s: (b ^ 1, s)),
        pairs(fourth),
    )


def held(x):
    return pltpu.with_memory_space_constraint(x, pltpu.VMEM)


def call(kernel, name, outs, *operands):
    whole = pl.BlockSpec(memory_space=pltpu.VMEM)
    flags = pl.BlockSpec(memory_space=pltpu.SMEM)
    return pl.pallas_call(
        kernel,
        in_specs=[flags] + [whole] * (len(operands) - 1),
        out_specs=[whole] * len(outs),
        out_shape=[pltpu.VMEM(shape, dtype) for shape, dtype in outs],
        compiler_params=pltpu.CompilerParams(vmem_limit_bytes=VMEM_BYTES),
        name=name,
    )(operands[0], *[held(x) for x in operands[1:]])


def start_all(copies):
    for copy in copies:
        copy.start()


def wait_all(copies):
    for copy in copies:
        copy.wait()


def cut_copies(first, one, two, out, sem, at):
    cut = pl.ds(first, out.shape[2])
    return [pltpu.make_async_copy(x.at[:, cut], out.at[i], sem.at[at + i]) for i, x in enumerate((one, two))]


def start_sends(first, polar, q, k, v, g, kv, chosen, sem):
    start_all(cut_copies(first, k, v, kv, sem, 0))
    pl.when(polar)(lambda: start_all(cut_copies(first, q, g, chosen, sem, 2)))
    pl.when(jnp.logical_not(polar))(lambda: start_all(cut_copies(first, k, v, chosen, sem, 2)))
    return cut_copies(first, k, v, kv, sem, 0) + cut_copies(first, k, v, chosen, sem, 2)


def is_polar(lat_count):
    b = lax.axis_index("lat")
    return (b == 0) | (b == lat_count - 1)


def first_pack_kernel(lat_count, q, k, v, g, kv, chosen, sem):
    wait_all(start_sends(0, is_polar(lat_count), q, k, v, g, kv, chosen, sem))


def later_pack_kernel(firsts, lat_count, lon_count, neighbours_in, partner_in, q, k, v, g, flags, *rest):
    *outs, sem, neighbours, partner = rest
    b, s = lax.axis_index("lat"), lax.axis_index("lon")
    polar = is_polar(lat_count)
    count = len(firsts)
    tables = [
        pltpu.make_async_copy(neighbours_in, neighbours, sem.at[0, 4]),
        pltpu.make_async_copy(partner_in, partner, sem.at[0, 5]),
    ]
    start_all(tables)
    copies = []
    for c in range(1, count):
        pair = outs[count + 2 * c - 2 : count + 2 * c]
        copies += start_sends(firsts[c], polar, q, k, v, g, *pair, sem.at[c])
    for c in range(count):
        more = cut_copies(firsts[c], q, g, outs[c], sem.at[c], 6)
        start_all(more)
        copies += more
    wait_all(tables)

    half = lon_count // 2
    ring = jnp.where(polar, half, lon_count)
    base = jnp.where(polar & (s >= half), half, 0)
    place = s - base
    second = base + lax.rem(place + jnp.where(lax.rem(place, 2) == 0, ring - 1, 1), ring)
    first = jnp.where(lax.rem(s, 2) == 0, s + 1, s - 1)
    even = lax.rem(b, 2) == 0
    third = jnp.where(even, b + 1, b - 1)
    fourth = jnp.where(even, b - 1, b + 1)
    slots = [
        b * lon_count + s,
        b * lon_count + first,
        b * lon_count + second,
        third * lon_count + s,
        jnp.where(polar, -7, fourth * lon_count + s),
    ]
    across = jnp.where(s >= half, s - half, s + half)
    pole = jnp.where(b == 0, 0, 1)

    def mark(strip, at, tiles):
        tile = b * lon_count + strip
        links = [neighbours[i, tile] for i in range(neighbours.shape[0])]
        links.append(jnp.where(polar, b * lon_count + partner[pole, strip], -9))
        for i, one in enumerate(tiles):
            flags[at + i] = functools.reduce(jnp.logical_or, [one == link for link in links]).astype(jnp.int32)

    mark(s, 0, slots)
    mark(across, 8, slots[:3])
    flags[7] = polar.astype(jnp.int32)
    for i in (5, 6, 11, 12, 13, 14, 15):
        flags[i] = 0
    wait_all(copies)


def pack(firsts, widths, lat_count, lon_count, neighbours, partner, q, k, v, g):
    tokens = q.shape[0]
    pairs = [pltpu.VMEM((2, tokens, wide), BF16) for wide in widths]
    smem, vmem, anywhere = [pl.BlockSpec(memory_space=m) for m in (pltpu.SMEM, pltpu.VMEM, pl.ANY)]
    far = [pltpu.with_memory_space_constraint(x, pltpu.HBM) for x in (neighbours, partner, q, k, v, g)]
    params = pltpu.CompilerParams(vmem_limit_bytes=VMEM_BYTES)
    kv, chosen = pl.pallas_call(
        functools.partial(first_pack_kernel, lat_count),
        in_specs=[anywhere] * 4,
        out_specs=[vmem] * 2,
        out_shape=[pairs[0]] * 2,
        scratch_shapes=[pltpu.SemaphoreType.DMA((4,))],
        compiler_params=params,
        name="first_pack",
    )(*far[2:])
    count = len(widths)
    later = [pair for pair in pairs[1:] for _ in range(2)]
    flags, *outs = pl.pallas_call(
        functools.partial(later_pack_kernel, firsts, lat_count, lon_count),
        in_specs=[anywhere] * 6,
        out_specs=[smem] + [vmem] * (count + len(later)),
        out_shape=[jax.ShapeDtypeStruct((16,), jnp.int32)] + pairs + later,
        scratch_shapes=[
            pltpu.SemaphoreType.DMA((count, 8)),
            pltpu.SMEM(neighbours.shape, jnp.int32),
            pltpu.SMEM(partner.shape, jnp.int32),
        ],
        compiler_params=params,
        name="later_pack",
    )(*far)
    sends = [(kv, chosen)] + [outs[count + 2 * c - 2 : count + 2 * c] for c in range(1, count)]
    return flags, [(sends[c][0], outs[c], sends[c][1]) for c in range(count)]


def after(x, *others):
    return lax.optimization_barrier((x, *others))[0]


def finish_kernel(flags, b4, b2, b3, b1, att, dq, dk, dv, *rest):
    o_att, o_dq, o_dk, o_dv = rest[-4:]
    inner = jnp.where(flags[7] > 0, 0.0, 1.0).astype(F32)
    fourth = [b4[i].astype(F32) for i in range(2)]
    o_att[...] = (att[...] + (1.0 - inner) * fourth[0]).astype(BF16)
    o_dq[...] = (SCALE * (dq[...] + (1.0 - inner) * fourth[1])).astype(BF16)
    terms = [b1[i].astype(F32) + b2[i].astype(F32) + b3[i].astype(F32) + inner * fourth[i] for i in range(2)]
    o_dk[...] = (SCALE * (dk[...] + terms[0])).astype(BF16)
    o_dv[...] = (dv[...] + terms[1]).astype(BF16)


def finish(first, features, flags, parts, returned, before):
    tokens, wide = parts[0].shape
    block = math.gcd(first, wide) if FINISH_WIDTH == 0 else math.gcd(FINISH_WIDTH * DH, math.gcd(first, wide))
    flat = pl.BlockSpec((tokens, block), lambda i: (0, i))
    pair = pl.BlockSpec((2, tokens, block), lambda i: (0, 0, i))
    place = pl.BlockSpec((tokens, block), lambda i: (0, first // block + i))
    kept = [pl.BlockSpec(memory_space=pl.ANY)] * len(before)
    return pl.pallas_call(
        finish_kernel,
        grid=(wide // block,),
        in_specs=[pl.BlockSpec(memory_space=pltpu.SMEM)] + [pair] * 4 + [flat] * 4 + kept,
        out_specs=[place] * 4,
        out_shape=[jax.ShapeDtypeStruct((tokens, features), BF16)] * 4,
        input_output_aliases={9 + i: i for i in range(len(before))},
        compiler_params=pltpu.CompilerParams(vmem_limit_bytes=VMEM_BYTES),
        name="finish",
    )(flags, *[returned[i] for i in (3, 1, 2, 0)], *parts, *before)


def body(queries, keys, values, out_grad, neighbours, partner):
    lat_count, lon_count = lax.axis_size("lat"), lax.axis_size("lon")
    tile_rows, tile_cols, features = queries.shape
    tokens = tile_rows * tile_cols
    heads = features // DH
    cuts = [heads * part // SHARES[-1] for part in SHARES]
    counts = [b - a for a, b in zip(cuts, cuts[1:])]
    firsts, widths = [a * DH for a in cuts[:-1]], [n * DH for n in counts]
    chunks = len(counts)
    q, k, v, g = [x.reshape(tokens, features) for x in (queries, keys, values, out_grad)]
    plan = exchange_plan(lon_count, lat_count)
    axes = ("lon", "lat")
    def exchange(operands, ties):
        out = [None] * 4
        for i in ORDER:
            out[i] = lax.ppermute(after(operands[i], *ties[i]) if ties[i] else operands[i], axes, plan[i])
        return out

    flags, packed = pack(firsts, widths, lat_count, lon_count, neighbours.T, partner, q, k, v, g)

    near = []
    for c in range(chunks):
        kv, qg, chosen = packed[c]
        ties = [[]] * 4 if c == 0 else [[near[-1][i] for i in tie] for tie in TIES]
        near.append(exchange((kv, kv, kv, chosen), ties))

    mine, theirs = [], []
    for c in range(chunks):
        kv, qg, chosen = packed[c]
        kernel = functools.partial(stats_kernel, counts[c], tokens)
        mine += call(kernel, "stats", [((-(-3 * counts[c] // 8) * 8, 2 * tokens), F32)], flags, *[near[c][i] for i in (3, 1, 2, 0)], qg, kv)
        theirs.append(lax.ppermute(mine[c], axes, plan[3]))
    done = []
    for c in range(chunks):
        kv, qg, chosen = packed[c]
        other = after(theirs[c], mine[c + 1]) if AHEAD and c + 1 < chunks else theirs[c]
        kernel = functools.partial(grads_kernel, counts[c], tokens)
        outs = [((tokens, widths[c]), F32)] * 4 + [((2, tokens, widths[c]), BF16)] * 4
        results = call(kernel, "grads", outs, flags, *[near[c][i] for i in (3, 1, 2, 0)], mine[c], other, qg, kv)
        if c + 1 < chunks:
            ties = [[theirs[c + 1]] if i in LATE else [] for i in range(4)]
        else:
            ties = [[done[-1][1][i] for i in tie] for tie in LAST]
        done.append((results[:4], exchange(results[4:], ties)))
    outs = []
    for c in range(chunks):
        outs = finish(firsts[c], features, flags, *done[c], outs)
    return tuple(x.reshape(tile_rows, tile_cols, features) for x in outs)


def solution(mesh):
    spec = P("lat", "lon", None)
    return jax.shard_map(
        body,
        mesh=mesh,
        in_specs=(spec,) * 4 + (P(),) * 2,
        out_specs=(spec,) * 4,
        check_vma=False,
    )
```

```python
import functools
import math

import jax
import jax.numpy as jnp
from jax import lax
from jax.experimental import pallas as pl
from jax.experimental.pallas import tpu as pltpu
from jax.sharding import PartitionSpec as P

DH = 128
SHARES = (0, 6, 12)
FINISH_HEADS = 3
ORDER = (3, 1, 2, 0)
TIES = ((3,), (0,), (3,), (0,))
LATE = (1, 1, 1, 1)
FIRST = (0, 0, 0, 0)
PIECES = 1
LAST = ((2,), (), (), ())
VMEM_BYTES = 16 * 1024 * 1024
SCALE = DH**-0.5
FACTOR = SCALE * math.log2(math.e)
LOW = -1e30
F32 = jnp.float32
BF16 = jnp.bfloat16


def dot_nt(a, b):
    return lax.dot_general(a, b, (((1,), (1,)), ((), ())), preferred_element_type=F32)


def dot_nn(a, b):
    return lax.dot_general(a, b, (((1,), (0,)), ((), ())), preferred_element_type=F32)


def dot_tn(a, b):
    return lax.dot_general(a, b, (((0,), (0,)), ((), ())), preferred_element_type=F32)


def rows(*parts):
    return jnp.concatenate(parts, axis=0)


def gathered(j, polar, qg, kv, near):
    cols = pl.ds(j * DH, DH)
    slots = (kv,) + (near[:3] if polar else near)
    kk, vv = [rows(*[r[i, :, cols] for r in slots]) for i in range(2)]
    qq, gg = [rows(qg[i, :, cols], near[3][i, :, cols]) if polar else qg[i, :, cols] for i in range(2)]
    return qq, gg, kk, vv


def is_polar(lat_count):
    b = lax.axis_index("lat")
    return (b == 0) | (b == lat_count - 1)


def by_band(lat_count, work):
    polar = is_polar(lat_count)
    pl.when(polar)(lambda: work(True))
    pl.when(jnp.logical_not(polar))(lambda: work(False))


def stats_kernel(lat_count, heads, tokens, bias_rows, n4, n2, n3, n1, qg, kv, out):
    near = (n1, n2, n3, n4)

    def work(polar):
        width = 2 * tokens if polar else tokens
        count = 4 if polar else 5
        bias = [bias_rows[b : b + 1, :width] for b in range(count)]
        tops, sums, deltas = [], [], []
        for j in range(heads):
            qq, gg, kk, vv = gathered(j, polar, qg, kv, near)
            s = dot_nt(kk, qq)
            dp = dot_nt(vv, gg)
            for b in range(count):
                part = s[b * tokens : (b + 1) * tokens]
                high = jnp.max(part, axis=0, keepdims=True) * FACTOR + bias[b]
                if b:
                    high = jnp.maximum(top, high)
                e = jnp.exp2((part * FACTOR + bias[b]) - high)
                one = jnp.sum(e, axis=0, keepdims=True)
                two = jnp.sum(e * dp[b * tokens : (b + 1) * tokens], axis=0, keepdims=True)
                if b:
                    fade = jnp.exp2(top - high)
                    one, two = total * fade + one, delta * fade + two
                top, total, delta = high, one, two
            tops.append(top)
            sums.append(total)
            deltas.append(delta)
        stat = rows(*tops, *sums, *deltas)
        for r in range(3 * heads):
            out[r : r + 1, :width] = stat[r : r + 1]
        if out.shape[0] > 3 * heads:
            out[3 * heads :, :] = jnp.zeros((out.shape[0] - 3 * heads, 2 * tokens), F32)
        if not polar:
            out[: 3 * heads, tokens:] = jnp.zeros((3 * heads, tokens), F32)

    by_band(lat_count, work)


def grads_kernel(lat_count, heads, tokens, bias_rows, n4, n2, n3, n1, mine, theirs, qg, kv, att, dq, dk, dv, r1, r2, r3, r4):
    near = (n1, n2, n3, n4)
    back = (r1, r2, r3, r4)

    def work(polar):
        width = 2 * tokens if polar else tokens
        count = 4 if polar else 5
        bias = [bias_rows[b : b + 1, :width] for b in range(count)]
        for j in range(heads):
            cols = pl.ds(j * DH, DH)
            top, total, delta = [mine[r * heads + j : r * heads + j + 1, :width] for r in range(3)]
            if polar:
                top2, total2, delta2 = [
                    jnp.concatenate(
                        [
                            theirs[r * heads + j : r * heads + j + 1, tokens:],
                            theirs[r * heads + j : r * heads + j + 1, :tokens],
                        ],
                        axis=1,
                    )
                    for r in range(3)
                ]
                high = jnp.maximum(top, top2)
                a1, a2 = jnp.exp2(top - high), jnp.exp2(top2 - high)
                total = total * a1 + total2 * a2
                delta = delta * a1 + delta2 * a2
                top = high
            lse = top + jnp.log2(total)
            delta = delta / total
            qq, gg, kk, vv = gathered(j, polar, qg, kv, near)
            s = dot_nt(kk, qq)
            dp = dot_nt(vv, gg)
            ps = []
            for b in range(count):
                ps.append(jnp.exp2(s[b * tokens : (b + 1) * tokens] * FACTOR + (bias[b] - lse)))
            p = rows(*ps)
            w = p.astype(BF16)
            ds = (p * (dp - delta)).astype(BF16)
            dkk = dot_nn(ds, qq)
            dvv = dot_nn(w, gg)
            o = dot_tn(vv, w).T
            dqq = dot_tn(kk, ds).T
            att[:, cols] = o[:tokens]
            dq[:, cols] = dqq[:tokens]
            dk[:, cols] = dkk[:tokens]
            dv[:, cols] = dvv[:tokens]
            for b in range(1, count):
                back[b - 1][0, :, cols] = dkk[b * tokens : (b + 1) * tokens].astype(BF16)
                back[b - 1][1, :, cols] = dvv[b * tokens : (b + 1) * tokens].astype(BF16)
            if polar:
                r4[0, :, cols] = o[tokens:].astype(BF16)
                r4[1, :, cols] = dqq[tokens:].astype(BF16)

    by_band(lat_count, work)


def exchange_plan(lon_count, lat_count):
    half = lon_count // 2

    def polar(b):
        return b == 0 or b == lat_count - 1

    def second(b, s):
        ring, base = (half, s // half * half) if polar(b) else (lon_count, 0)
        place = s - base
        return base + (place - 1 if place % 2 == 0 else place + 1) % ring

    def fourth(b, s):
        if polar(b):
            return b, (s + half) % lon_count
        return (b - 1 if b % 2 == 0 else b + 1), s

    cells = [(b, s) for b in range(lat_count) for s in range(lon_count)]

    def pairs(move):
        return [(s * lat_count + b, move(b, s)[1] * lat_count + move(b, s)[0]) for b, s in cells]

    return (
        pairs(lambda b, s: (b, s ^ 1)),
        pairs(lambda b, s: (b, second(b, s))),
        pairs(lambda b, s: (b ^ 1, s)),
        pairs(fourth),
    )


def held(x):
    return pltpu.with_memory_space_constraint(x, pltpu.VMEM)


def call(kernel, name, outs, *operands):
    whole = pl.BlockSpec(memory_space=pltpu.VMEM)
    return pl.pallas_call(
        kernel,
        in_specs=[whole] * len(operands),
        out_specs=[whole] * len(outs),
        out_shape=[pltpu.VMEM(shape, dtype) for shape, dtype in outs],
        compiler_params=pltpu.CompilerParams(vmem_limit_bytes=VMEM_BYTES),
        name=name,
    )(*[held(x) for x in operands])


def start_all(copies):
    for copy in copies:
        copy.start()


def wait_all(copies):
    for copy in copies:
        copy.wait()


def cut_copies(first, one, two, out, sem, at):
    cut = pl.ds(first, out.shape[2])
    tall = out.shape[1] // PIECES
    parts = [pl.ds(i * tall, tall) for i in range(PIECES)]
    return [
        pltpu.make_async_copy(x.at[part, cut], out.at[i, part], sem.at[at + i])
        for i, x in enumerate((one, two))
        for part in parts
    ]


def start_sends(first, polar, q, k, v, g, kv, chosen, sem):
    start_all(cut_copies(first, k, v, kv, sem, 0))
    pl.when(polar)(lambda: start_all(cut_copies(first, q, g, chosen, sem, 2)))
    pl.when(jnp.logical_not(polar))(lambda: start_all(cut_copies(first, k, v, chosen, sem, 2)))
    return cut_copies(first, k, v, kv, sem, 0) + cut_copies(first, k, v, chosen, sem, 2)


def first_pack_kernel(lat_count, q, k, v, g, kv, chosen, sem):
    wait_all(start_sends(0, is_polar(lat_count), q, k, v, g, kv, chosen, sem))


def later_pack_kernel(firsts, lat_count, lon_count, neighbours_in, partner_in, q, k, v, g, bias, *rest):
    *outs, sem, neighbours, partner = rest
    b, s = lax.axis_index("lat"), lax.axis_index("lon")
    polar = is_polar(lat_count)
    count = len(firsts)
    tables = [
        pltpu.make_async_copy(neighbours_in, neighbours, sem.at[0, 4]),
        pltpu.make_async_copy(partner_in, partner, sem.at[0, 5]),
    ]
    start_all(tables)
    copies = []
    for c in range(1, count):
        pair = outs[count + 2 * c - 2 : count + 2 * c]
        copies += start_sends(firsts[c], polar, q, k, v, g, *pair, sem.at[c])
    for c in range(count):
        more = cut_copies(firsts[c], q, g, outs[c], sem.at[c], 6)
        start_all(more)
        copies += more
    wait_all(tables)

    half = lon_count // 2
    ring = jnp.where(polar, half, lon_count)
    base = jnp.where(polar & (s >= half), half, 0)
    place = s - base
    second = base + lax.rem(place + jnp.where(lax.rem(place, 2) == 0, ring - 1, 1), ring)
    first = jnp.where(lax.rem(s, 2) == 0, s + 1, s - 1)
    even = lax.rem(b, 2) == 0
    third = jnp.where(even, b + 1, b - 1)
    fourth = jnp.where(even, b - 1, b + 1)
    slots = [
        b * lon_count + s,
        b * lon_count + first,
        b * lon_count + second,
        third * lon_count + s,
        jnp.where(polar, -7, fourth * lon_count + s),
    ]
    across = jnp.where(s >= half, s - half, s + half)
    pole = jnp.where(b == 0, 0, 1)

    def linked(strip, tiles):
        tile = b * lon_count + strip
        links = [neighbours[i, tile] for i in range(neighbours.shape[0])]
        links.append(jnp.where(polar, b * lon_count + partner[pole, strip], -9))
        found = [functools.reduce(jnp.logical_or, [one == link for link in links]) for one in tiles]
        return [jnp.where(x, 0.0, LOW).astype(F32) for x in found]

    own, other = linked(s, slots), linked(across, slots[:3])
    lane = lax.broadcasted_iota(jnp.int32, (1, bias.shape[1]), 1)
    for i in range(bias.shape[0]):
        row = [x[i] if i < len(x) else jnp.float32(LOW) for x in (own, other)]
        bias[i : i + 1, :] = jnp.where(lane < bias.shape[1] // 2, row[0], row[1])
    wait_all(copies)


def pack(firsts, widths, lat_count, lon_count, neighbours, partner, q, k, v, g):
    tokens = q.shape[0]
    pairs = [pltpu.VMEM((2, tokens, wide), BF16) for wide in widths]
    vmem, anywhere = [pl.BlockSpec(memory_space=m) for m in (pltpu.VMEM, pl.ANY)]
    far = [pltpu.with_memory_space_constraint(x, pltpu.HBM) for x in (neighbours, partner, q, k, v, g)]
    params = pltpu.CompilerParams(vmem_limit_bytes=VMEM_BYTES)
    kv, chosen = pl.pallas_call(
        functools.partial(first_pack_kernel, lat_count),
        in_specs=[anywhere] * 4,
        out_specs=[vmem] * 2,
        out_shape=[pairs[0]] * 2,
        scratch_shapes=[pltpu.SemaphoreType.DMA((4,))],
        compiler_params=params,
        name="first_pack",
    )(*far[2:])
    count = len(widths)
    later = [pair for pair in pairs[1:] for _ in range(2)]
    bias, *outs = pl.pallas_call(
        functools.partial(later_pack_kernel, firsts, lat_count, lon_count),
        in_specs=[anywhere] * 6,
        out_specs=[vmem] * (1 + count + len(later)),
        out_shape=[pltpu.VMEM((8, 2 * tokens), F32)] + pairs + later,
        scratch_shapes=[
            pltpu.SemaphoreType.DMA((count, 8)),
            pltpu.SMEM(neighbours.shape, jnp.int32),
            pltpu.SMEM(partner.shape, jnp.int32),
        ],
        compiler_params=params,
        name="later_pack",
    )(*far)
    sends = [(kv, chosen)] + [outs[count + 2 * c - 2 : count + 2 * c] for c in range(1, count)]
    return bias, [(sends[c][0], outs[c], sends[c][1]) for c in range(count)]


def after(x, *others):
    return lax.optimization_barrier((x, *others))[0]


def finish_kernel(lat_count, first, step, b4, b2, b3, b1, att, dq, dk, dv, *rest):
    outs, (made, sem) = rest[-6:-2], rest[-2:]
    inner = jnp.where(is_polar(lat_count), 0.0, 1.0).astype(F32)
    wide = att.shape[1]
    copies = []
    for i in range(wide // step):
        cols = pl.ds(i * step, step)
        fourth = [b4[j, :, cols].astype(F32) for j in range(2)]
        terms = [sum(b[j, :, cols].astype(F32) for b in (b1, b2, b3)) + inner * fourth[j] for j in range(2)]
        made[0, :, cols] = (att[:, cols] + (1.0 - inner) * fourth[0]).astype(BF16)
        made[1, :, cols] = (SCALE * (dq[:, cols] + (1.0 - inner) * fourth[1])).astype(BF16)
        made[2, :, cols] = (SCALE * (dk[:, cols] + terms[0])).astype(BF16)
        made[3, :, cols] = (dv[:, cols] + terms[1]).astype(BF16)
        for j in range(4):
            place = outs[j].at[:, pl.ds(first + i * step, step)]
            copies.append(pltpu.make_async_copy(made.at[j, :, cols], place, sem.at[i, j]))
            copies[-1].start()
    wait_all(copies)


def finish(lat_count, first, features, parts, returned, before):
    tokens, wide = parts[0].shape
    step = DH * math.gcd(wide // DH, FINISH_HEADS)
    vmem, anywhere = [pl.BlockSpec(memory_space=m) for m in (pltpu.VMEM, pl.ANY)]
    near = [held(x) for x in (*[returned[i] for i in (3, 1, 2, 0)], *parts)]
    return pl.pallas_call(
        functools.partial(finish_kernel, lat_count, first, step),
        in_specs=[vmem] * 8 + [anywhere] * len(before),
        out_specs=[anywhere] * 4,
        out_shape=[jax.ShapeDtypeStruct((tokens, features), BF16)] * 4,
        input_output_aliases={8 + i: i for i in range(len(before))},
        scratch_shapes=[pltpu.VMEM((4, tokens, wide), BF16), pltpu.SemaphoreType.DMA((wide // step, 4))],
        compiler_params=pltpu.CompilerParams(vmem_limit_bytes=VMEM_BYTES),
        name="finish",
    )(*near, *before)


def body(queries, keys, values, out_grad, neighbours, partner):
    lat_count, lon_count = lax.axis_size("lat"), lax.axis_size("lon")
    tile_rows, tile_cols, features = queries.shape
    tokens = tile_rows * tile_cols
    heads = features // DH
    cuts = [heads * part // SHARES[-1] for part in SHARES]
    counts = [b - a for a, b in zip(cuts, cuts[1:])]
    firsts, widths = [a * DH for a in cuts[:-1]], [n * DH for n in counts]
    chunks = len(counts)
    q, k, v, g = [x.reshape(tokens, features) for x in (queries, keys, values, out_grad)]
    plan = exchange_plan(lon_count, lat_count)
    axes = ("lon", "lat")
    def exchange(operands, ties):
        out = [None] * 4
        for i in ORDER:
            out[i] = lax.ppermute(after(operands[i], *ties[i]) if ties[i] else operands[i], axes, plan[i])
        return out

    bias, packed = pack(firsts, widths, lat_count, lon_count, neighbours.T, partner, q, k, v, g)

    near = []
    for c in range(chunks):
        kv, qg, chosen = packed[c]
        ties = [[bias] * i for i in FIRST] if c == 0 else [[near[-1][i] for i in tie] for tie in TIES]
        near.append(exchange((kv, kv, kv, chosen), ties))

    def statistics(c, ties=()):
        kv, qg, chosen = packed[c]
        kernel = functools.partial(stats_kernel, lat_count, counts[c], tokens)
        outs = [((-(-3 * counts[c] // 8) * 8, 2 * tokens), F32)]
        mine.extend(call(kernel, "stats", outs, after(bias, *ties), *[near[c][i] for i in (3, 1, 2, 0)], qg, kv))
        theirs.append(lax.ppermute(mine[c], axes, plan[3]))

    def gradients(c):
        kv, qg, chosen = packed[c]
        kernel = functools.partial(grads_kernel, lat_count, counts[c], tokens)
        outs = [((tokens, widths[c]), F32)] * 4 + [((2, tokens, widths[c]), BF16)] * 4
        return call(kernel, "grads", outs, bias, *[near[c][i] for i in (3, 1, 2, 0)], mine[c], theirs[c], qg, kv)

    mine, theirs, done = [], [], []
    statistics(0)
    for c in range(chunks):
        results = gradients(c)
        ties = [[]] * 4
        if c + 1 < chunks:
            statistics(c + 1, results[:1])
            ties = [[mine[c + 1]] * (LATE[i] == 1) + [theirs[c + 1]] * (LATE[i] == 2) for i in range(4)]
        if c > 0:
            ties = [ties[i] + [done[-1][1][j] for j in LAST[i]] for i in range(4)]
        done.append((results[:4], exchange(results[4:], ties)))
    outs = []
    for c in range(chunks):
        outs = finish(lat_count, firsts[c], features, *done[c], outs)
    return tuple(x.reshape(tile_rows, tile_cols, features) for x in outs)


def solution(mesh):
    spec = P("lat", "lon", None)
    return jax.shard_map(
        body,
        mesh=mesh,
        in_specs=(spec,) * 4 + (P(),) * 2,
        out_specs=(spec,) * 4,
        check_vma=False,
    )
```

```python
import functools
import math

import jax
import jax.numpy as jnp
from jax import lax
from jax.experimental import pallas as pl
from jax.experimental.pallas import tpu as pltpu
from jax.sharding import PartitionSpec as P

DH = 128
SHARES = (0, 6, 12)
ORDER = (3, 1, 2, 0)
TIES = ((3,), (0,), (3,), (0,))
LATE = (1, 1, 1, 1)
FIRST = (0, 0, 0, 0)
PIECES = 1
LAST = ((2,), (), (), ())
VMEM_BYTES = 16 * 1024 * 1024
SCALE = DH**-0.5
FACTOR = SCALE * math.log2(math.e)
LOW = -1e30
F32 = jnp.float32
BF16 = jnp.bfloat16


def dot_nt(a, b):
    return lax.dot_general(a, b, (((1,), (1,)), ((), ())), preferred_element_type=F32)


def dot_nn(a, b):
    return lax.dot_general(a, b, (((1,), (0,)), ((), ())), preferred_element_type=F32)


def dot_tn(a, b):
    return lax.dot_general(a, b, (((0,), (0,)), ((), ())), preferred_element_type=F32)


def rows(*parts):
    return jnp.concatenate(parts, axis=0)


def gathered(j, polar, qg, kv, near):
    cols = pl.ds(j * DH, DH)
    slots = (kv,) + (near[:3] if polar else near)
    kk, vv = [rows(*[r[i, :, cols] for r in slots]) for i in range(2)]
    qq, gg = [rows(qg[i, :, cols], near[3][i, :, cols]) if polar else qg[i, :, cols] for i in range(2)]
    return qq, gg, kk, vv


def is_polar(lat_count):
    b = lax.axis_index("lat")
    return (b == 0) | (b == lat_count - 1)


def by_band(lat_count, work):
    polar = is_polar(lat_count)
    pl.when(polar)(lambda: work(True))
    pl.when(jnp.logical_not(polar))(lambda: work(False))


def stats_kernel(lat_count, heads, tokens, bias_rows, n4, n2, n3, n1, qg, kv, out):
    near = (n1, n2, n3, n4)

    def work(polar):
        width = 2 * tokens if polar else tokens
        count = 4 if polar else 5
        bias = [bias_rows[b : b + 1, :width] for b in range(count)]
        tops, sums, deltas = [], [], []
        for j in range(heads):
            qq, gg, kk, vv = gathered(j, polar, qg, kv, near)
            s = dot_nt(kk, qq)
            dp = dot_nt(vv, gg)
            for b in range(count):
                part = s[b * tokens : (b + 1) * tokens]
                high = jnp.max(part, axis=0, keepdims=True) * FACTOR + bias[b]
                if b:
                    high = jnp.maximum(top, high)
                e = jnp.exp2((part * FACTOR + bias[b]) - high)
                one = jnp.sum(e, axis=0, keepdims=True)
                two = jnp.sum(e * dp[b * tokens : (b + 1) * tokens], axis=0, keepdims=True)
                if b:
                    fade = jnp.exp2(top - high)
                    one, two = total * fade + one, delta * fade + two
                top, total, delta = high, one, two
            tops.append(top)
            sums.append(total)
            deltas.append(delta)
        stat = rows(*tops, *sums, *deltas)
        for r in range(3 * heads):
            out[r : r + 1, :width] = stat[r : r + 1]
        if out.shape[0] > 3 * heads:
            out[3 * heads :, :] = jnp.zeros((out.shape[0] - 3 * heads, 2 * tokens), F32)
        if not polar:
            out[: 3 * heads, tokens:] = jnp.zeros((3 * heads, tokens), F32)

    by_band(lat_count, work)


def grads_kernel(lat_count, heads, tokens, bias_rows, n4, n2, n3, n1, mine, theirs, qg, kv, att, dq, dk, dv, r1, r2, r3, r4):
    near = (n1, n2, n3, n4)
    back = (r1, r2, r3, r4)

    def work(polar):
        width = 2 * tokens if polar else tokens
        count = 4 if polar else 5
        bias = [bias_rows[b : b + 1, :width] for b in range(count)]
        for j in range(heads):
            cols = pl.ds(j * DH, DH)
            top, total, delta = [mine[r * heads + j : r * heads + j + 1, :width] for r in range(3)]
            if polar:
                top2, total2, delta2 = [
                    jnp.concatenate(
                        [
                            theirs[r * heads + j : r * heads + j + 1, tokens:],
                            theirs[r * heads + j : r * heads + j + 1, :tokens],
                        ],
                        axis=1,
                    )
                    for r in range(3)
                ]
                high = jnp.maximum(top, top2)
                a1, a2 = jnp.exp2(top - high), jnp.exp2(top2 - high)
                total = total * a1 + total2 * a2
                delta = delta * a1 + delta2 * a2
                top = high
            lse = top + jnp.log2(total)
            delta = delta / total
            qq, gg, kk, vv = gathered(j, polar, qg, kv, near)
            s = dot_nt(kk, qq)
            dp = dot_nt(vv, gg)
            ps = []
            for b in range(count):
                ps.append(jnp.exp2(s[b * tokens : (b + 1) * tokens] * FACTOR + (bias[b] - lse)))
            p = rows(*ps)
            w = p.astype(BF16)
            ds = (p * (dp - delta)).astype(BF16)
            dkk = dot_nn(ds, qq)
            dvv = dot_nn(w, gg)
            o = dot_tn(vv, w).T
            dqq = dot_tn(kk, ds).T
            att[:, cols] = o[:tokens]
            dq[:, cols] = dqq[:tokens]
            dk[:, cols] = dkk[:tokens]
            dv[:, cols] = dvv[:tokens]
            for b in range(1, count):
                back[b - 1][0, :, cols] = dkk[b * tokens : (b + 1) * tokens].astype(BF16)
                back[b - 1][1, :, cols] = dvv[b * tokens : (b + 1) * tokens].astype(BF16)
            if polar:
                r4[0, :, cols] = o[tokens:].astype(BF16)
                r4[1, :, cols] = dqq[tokens:].astype(BF16)

    by_band(lat_count, work)


def exchange_plan(lon_count, lat_count):
    half = lon_count // 2

    def polar(b):
        return b == 0 or b == lat_count - 1

    def second(b, s):
        ring, base = (half, s // half * half) if polar(b) else (lon_count, 0)
        place = s - base
        return base + (place - 1 if place % 2 == 0 else place + 1) % ring

    def fourth(b, s):
        if polar(b):
            return b, (s + half) % lon_count
        return (b - 1 if b % 2 == 0 else b + 1), s

    cells = [(b, s) for b in range(lat_count) for s in range(lon_count)]

    def pairs(move):
        return [(s * lat_count + b, move(b, s)[1] * lat_count + move(b, s)[0]) for b, s in cells]

    return (
        pairs(lambda b, s: (b, s ^ 1)),
        pairs(lambda b, s: (b, second(b, s))),
        pairs(lambda b, s: (b ^ 1, s)),
        pairs(fourth),
    )


def held(x):
    return pltpu.with_memory_space_constraint(x, pltpu.VMEM)


def call(kernel, name, outs, *operands):
    whole = pl.BlockSpec(memory_space=pltpu.VMEM)
    return pl.pallas_call(
        kernel,
        in_specs=[whole] * len(operands),
        out_specs=[whole] * len(outs),
        out_shape=[pltpu.VMEM(shape, dtype) for shape, dtype in outs],
        compiler_params=pltpu.CompilerParams(vmem_limit_bytes=VMEM_BYTES),
        name=name,
    )(*[held(x) for x in operands])


def start_all(copies):
    for copy in copies:
        copy.start()


def wait_all(copies):
    for copy in copies:
        copy.wait()


def cut_copies(first, one, two, out, sem, at):
    cut = pl.ds(first, out.shape[2])
    tall = out.shape[1] // PIECES
    parts = [pl.ds(i * tall, tall) for i in range(PIECES)]
    return [
        pltpu.make_async_copy(x.at[part, cut], out.at[i, part], sem.at[at + i])
        for i, x in enumerate((one, two))
        for part in parts
    ]


def start_sends(first, polar, q, k, v, g, kv, chosen, sem):
    start_all(cut_copies(first, k, v, kv, sem, 0))
    pl.when(polar)(lambda: start_all(cut_copies(first, q, g, chosen, sem, 2)))
    pl.when(jnp.logical_not(polar))(lambda: start_all(cut_copies(first, k, v, chosen, sem, 2)))
    return cut_copies(first, k, v, kv, sem, 0) + cut_copies(first, k, v, chosen, sem, 2)


def first_pack_kernel(lat_count, q, k, v, g, kv, chosen, sem):
    wait_all(start_sends(0, is_polar(lat_count), q, k, v, g, kv, chosen, sem))


def later_pack_kernel(firsts, lat_count, lon_count, neighbours_in, partner_in, q, k, v, g, bias, *rest):
    *outs, sem, neighbours, partner = rest
    b, s = lax.axis_index("lat"), lax.axis_index("lon")
    polar = is_polar(lat_count)
    count = len(firsts)
    tables = [
        pltpu.make_async_copy(neighbours_in, neighbours, sem.at[0, 4]),
        pltpu.make_async_copy(partner_in, partner, sem.at[0, 5]),
    ]
    start_all(tables)
    copies = []
    for c in range(1, count):
        pair = outs[count + 2 * c - 2 : count + 2 * c]
        copies += start_sends(firsts[c], polar, q, k, v, g, *pair, sem.at[c])
    for c in range(count):
        more = cut_copies(firsts[c], q, g, outs[c], sem.at[c], 6)
        start_all(more)
        copies += more
    wait_all(tables)

    half = lon_count // 2
    ring = jnp.where(polar, half, lon_count)
    base = jnp.where(polar & (s >= half), half, 0)
    place = s - base
    second = base + lax.rem(place + jnp.where(lax.rem(place, 2) == 0, ring - 1, 1), ring)
    first = jnp.where(lax.rem(s, 2) == 0, s + 1, s - 1)
    even = lax.rem(b, 2) == 0
    third = jnp.where(even, b + 1, b - 1)
    fourth = jnp.where(even, b - 1, b + 1)
    slots = [
        b * lon_count + s,
        b * lon_count + first,
        b * lon_count + second,
        third * lon_count + s,
        jnp.where(polar, -7, fourth * lon_count + s),
    ]
    across = jnp.where(s >= half, s - half, s + half)
    pole = jnp.where(b == 0, 0, 1)

    def linked(strip, tiles):
        tile = b * lon_count + strip
        links = [neighbours[i, tile] for i in range(neighbours.shape[0])]
        links.append(jnp.where(polar, b * lon_count + partner[pole, strip], -9))
        found = [functools.reduce(jnp.logical_or, [one == link for link in links]) for one in tiles]
        return [jnp.where(x, 0.0, LOW).astype(F32) for x in found]

    own, other = linked(s, slots), linked(across, slots[:3])
    lane = lax.broadcasted_iota(jnp.int32, (1, bias.shape[1]), 1)
    for i in range(bias.shape[0]):
        row = [x[i] if i < len(x) else jnp.float32(LOW) for x in (own, other)]
        bias[i : i + 1, :] = jnp.where(lane < bias.shape[1] // 2, row[0], row[1])
    wait_all(copies)


def pack(firsts, widths, lat_count, lon_count, neighbours, partner, q, k, v, g):
    tokens = q.shape[0]
    pairs = [pltpu.VMEM((2, tokens, wide), BF16) for wide in widths]
    vmem, anywhere = [pl.BlockSpec(memory_space=m) for m in (pltpu.VMEM, pl.ANY)]
    far = [pltpu.with_memory_space_constraint(x, pltpu.HBM) for x in (neighbours, partner, q, k, v, g)]
    params = pltpu.CompilerParams(vmem_limit_bytes=VMEM_BYTES)
    kv, chosen = pl.pallas_call(
        functools.partial(first_pack_kernel, lat_count),
        in_specs=[anywhere] * 4,
        out_specs=[vmem] * 2,
        out_shape=[pairs[0]] * 2,
        scratch_shapes=[pltpu.SemaphoreType.DMA((4,))],
        compiler_params=params,
        name="first_pack",
    )(*far[2:])
    count = len(widths)
    later = [pair for pair in pairs[1:] for _ in range(2)]
    bias, *outs = pl.pallas_call(
        functools.partial(later_pack_kernel, firsts, lat_count, lon_count),
        in_specs=[anywhere] * 6,
        out_specs=[vmem] * (1 + count + len(later)),
        out_shape=[pltpu.VMEM((8, 2 * tokens), F32)] + pairs + later,
        scratch_shapes=[
            pltpu.SemaphoreType.DMA((count, 8)),
            pltpu.SMEM(neighbours.shape, jnp.int32),
            pltpu.SMEM(partner.shape, jnp.int32),
        ],
        compiler_params=params,
        name="later_pack",
    )(*far)
    sends = [(kv, chosen)] + [outs[count + 2 * c - 2 : count + 2 * c] for c in range(1, count)]
    return bias, [(sends[c][0], outs[c], sends[c][1]) for c in range(count)]


def after(x, *others):
    return lax.optimization_barrier((x, *others))[0]


def send_out(made, values, outs, cut, sem):
    for j, value in enumerate(values):
        made[j] = value.astype(BF16)
        pltpu.make_async_copy(made.at[j], outs[j].at[:, cut], sem.at[j]).start()
    for j in range(2):
        pltpu.make_async_copy(made.at[j], outs[j].at[:, cut], sem.at[j]).wait()


def early_finish_kernel(lat_count, first, b2, b3, b1, att, dq, dk, dv, *rest):
    outs, (kept, made, sem) = rest[-7:-3], rest[-3:]
    cut = pl.ds(first, att.shape[1])
    terms = [sum(b[j].astype(F32) for b in (b1, b2, b3)) for j in range(2)]
    keys, vals = dk[...] + terms[0], dv[...] + terms[1]

    def work(polar):
        if polar:
            kept[0], kept[1] = att[...], dq[...]
            send_out(made, (SCALE * keys, vals), outs[2:], cut, sem)
        else:
            kept[0], kept[1] = keys, vals
            send_out(made, (att[...], SCALE * dq[...]), outs[:2], cut, sem)

    by_band(lat_count, work)


def late_finish_kernel(lat_count, first, b4, kept, *rest):
    outs, (made, sem) = rest[-6:-2], rest[-2:]
    cut = pl.ds(first, b4.shape[2])
    one, two = [kept[j] + b4[j].astype(F32) for j in range(2)]

    def work(polar):
        if polar:
            send_out(made, (one, SCALE * two), outs[:2], cut, sem)
        else:
            send_out(made, (SCALE * one, two), outs[2:], cut, sem)

    by_band(lat_count, work)


def finish(lat_count, first, features, parts, returned, before):
    tokens, wide = parts[0].shape
    vmem, anywhere = [pl.BlockSpec(memory_space=m) for m in (pltpu.VMEM, pl.ANY)]
    whole = jax.ShapeDtypeStruct((tokens, features), BF16)

    def run(kernel, name, near, before, extra):
        return pl.pallas_call(
            functools.partial(kernel, lat_count, first),
            in_specs=[vmem] * len(near) + [anywhere] * len(before),
            out_specs=[anywhere] * 4 + [vmem] * len(extra),
            out_shape=[whole] * 4 + extra,
            input_output_aliases={len(near) + i: i for i in range(len(before))},
            scratch_shapes=[pltpu.VMEM((2, tokens, wide), BF16), pltpu.SemaphoreType.DMA((2,))],
            compiler_params=pltpu.CompilerParams(vmem_limit_bytes=VMEM_BYTES),
            name=name,
        )(*[held(x) for x in near], *before)

    near = [returned[i] for i in (1, 2, 0)] + list(parts)
    *outs, kept = run(early_finish_kernel, "early_finish", near, before, [pltpu.VMEM((2, tokens, wide), F32)])
    return run(late_finish_kernel, "late_finish", [returned[3], kept], outs, [])


def body(queries, keys, values, out_grad, neighbours, partner):
    lat_count, lon_count = lax.axis_size("lat"), lax.axis_size("lon")
    tile_rows, tile_cols, features = queries.shape
    tokens = tile_rows * tile_cols
    heads = features // DH
    cuts = [heads * part // SHARES[-1] for part in SHARES]
    counts = [b - a for a, b in zip(cuts, cuts[1:])]
    firsts, widths = [a * DH for a in cuts[:-1]], [n * DH for n in counts]
    chunks = len(counts)
    q, k, v, g = [x.reshape(tokens, features) for x in (queries, keys, values, out_grad)]
    plan = exchange_plan(lon_count, lat_count)
    axes = ("lon", "lat")
    def exchange(operands, ties):
        out = [None] * 4
        for i in ORDER:
            out[i] = lax.ppermute(after(operands[i], *ties[i]) if ties[i] else operands[i], axes, plan[i])
        return out

    bias, packed = pack(firsts, widths, lat_count, lon_count, neighbours.T, partner, q, k, v, g)

    near = []
    for c in range(chunks):
        kv, qg, chosen = packed[c]
        ties = [[bias] * i for i in FIRST] if c == 0 else [[near[-1][i] for i in tie] for tie in TIES]
        near.append(exchange((kv, kv, kv, chosen), ties))

    def statistics(c, ties=()):
        kv, qg, chosen = packed[c]
        kernel = functools.partial(stats_kernel, lat_count, counts[c], tokens)
        outs = [((-(-3 * counts[c] // 8) * 8, 2 * tokens), F32)]
        mine.extend(call(kernel, "stats", outs, after(bias, *ties), *[near[c][i] for i in (3, 1, 2, 0)], qg, kv))
        theirs.append(lax.ppermute(mine[c], axes, plan[3]))

    def gradients(c):
        kv, qg, chosen = packed[c]
        kernel = functools.partial(grads_kernel, lat_count, counts[c], tokens)
        outs = [((tokens, widths[c]), F32)] * 4 + [((2, tokens, widths[c]), BF16)] * 4
        return call(kernel, "grads", outs, bias, *[near[c][i] for i in (3, 1, 2, 0)], mine[c], theirs[c], qg, kv)

    mine, theirs, done = [], [], []
    statistics(0)
    for c in range(chunks):
        results = gradients(c)
        ties = [[]] * 4
        if c + 1 < chunks:
            statistics(c + 1, results[:1])
            ties = [[mine[c + 1]] * (LATE[i] == 1) + [theirs[c + 1]] * (LATE[i] == 2) for i in range(4)]
        if c > 0:
            ties = [ties[i] + [done[-1][1][j] for j in LAST[i]] for i in range(4)]
        done.append((results[:4], exchange(results[4:], ties)))
    outs = []
    for c in range(chunks):
        outs = finish(lat_count, firsts[c], features, *done[c], outs)
    return tuple(x.reshape(tile_rows, tile_cols, features) for x in outs)


def solution(mesh):
    spec = P("lat", "lon", None)
    return jax.shard_map(
        body,
        mesh=mesh,
        in_specs=(spec,) * 4 + (P(),) * 2,
        out_specs=(spec,) * 4,
        check_vma=False,
    )
```
